32 devices in a mesh: dev: 8 (over y, x, core), ta: 4 (over z).
Axes of the slice: x: 2, y: 2, z: 4, core: 2. Of those that a mesh axis runs over, the one named last changes fastest.
Arguments:
- tokens: bfloat16 [4, 16, 144, 384], P('ta', 'dev'), may hold values from -36 to 36
- out_grad: bfloat16 [4, 16, 144, 384], P('ta', 'dev'), may hold values from -6 to 6
- first_gain: float32 [384], replicated, may hold values from 0.25 to 1.75
- depth_qkv: bfloat16 [384, 1152], replicated, may hold values from -0.3125 to 0.3125
- depth_out: bfloat16 [384, 384], replicated, may hold values from -0.3125 to 0.3125
- time_qkv: bfloat16 [384, 1152], replicated, may hold values from -0.3125 to 0.3125
- time_out: bfloat16 [384, 384], replicated, may hold values from -0.3125 to 0.3125
- second_gain: float32 [384], replicated, may hold values from 0.25 to 1.75
- up_weight: bfloat16 [384, 1536], replicated, may hold values from -0.3125 to 0.3125
- spatial_kernel: float32 [3, 3, 3, 1536], replicated, may hold values from -1.25 to 1.25
- down_weight: bfloat16 [1536, 384], replicated, may hold values from -0.15625 to 0.15625
- depth_scale: float32 [6], replicated, may hold values from 2 to 10
- time_scale: float32 [6], replicated, may hold values from 2 to 10
Outputs:
- block_out: bfloat16 [4, 16, 144, 384], P('ta', 'dev')
- input_grad: bfloat16 [4, 16, 144, 384], P('ta', 'dev')
- depth_qkv_grad: float32 [384, 1152], replicated
- depth_out_grad: float32 [384, 384], replicated
- time_qkv_grad: float32 [384, 1152], replicated
- time_out_grad: float32 [384, 384], replicated
- up_grad: float32 [384, 1536], replicated
- kernel_grad: float32 [3, 3, 3, 1536], replicated
- down_grad: float32 [1536, 384], replicated
- first_gain_grad: float32 [384], replicated
- second_gain_grad: float32 [384], replicated
- depth_scale_grad: float32 [6], replicated
- time_scale_grad: float32 [6], replicated
The draws below stay inside these ranges and needn't reach their ends.
All inputs are finite; a program needn't handle non-finite values.
Results may differ from the reference program's by a relative error of at most 0.015.
Values may be sent and summed in bfloat16 or wider, within the bound.
A program may use at most 128 MiB of HBM per device.

```python
import math
import jax
import jax.numpy as jnp
from jax import lax

C = 384
NH = 6
HID = 1536
PH = 6
PW = 24
CELLS = 144
DEPTH = 16
FRAMES = 4


def draw_tokens(key, part):
    key_base, key_rows, key_cols = jax.random.split(key, 3)
    shape = (FRAMES, DEPTH, PH * PW, C)
    row_scale = jnp.exp(jax.random.uniform(key_rows, (FRAMES, DEPTH, PH * PW, 1), jnp.float32, math.log(0.3), math.log(3.0)))
    col_scale = jnp.exp(jax.random.uniform(key_cols, (C,), jnp.float32, math.log(0.3), math.log(3.0)))
    base = jax.random.normal(key_base, shape, jnp.float32)
    base = jnp.clip(base, -4.0, 4.0)
    return (base * row_scale * col_scale).astype(jnp.bfloat16)


def steps_of(own_key, dims, pieces, least, largest):
    def one(dim, blocks):
        steps = jax.random.uniform(jax.random.fold_in(jax.random.fold_in(own_key, 6), dim), (blocks,), jnp.float32, least / len(pieces), largest / len(pieces))
        return jnp.repeat(jnp.exp(steps), dims[dim] // blocks).reshape((-1,) + (1,) * (len(dims) - dim - 1))

    loudness = one(*pieces[0])
    for cut in pieces[1:]:
        loudness = loudness * one(*cut)
    return loudness


def scatter_about(stream_key, shape, scale, limit, pieces=(), kind=jnp.bfloat16):
    array = jax.random.normal(stream_key, shape, jnp.float32) * scale
    if len(pieces) > 0:
        array = steps_of(stream_key, shape, pieces, -0.22, 0.18) * array
    return jnp.clip(array, min=-limit, max=limit).astype(kind)


def setup_inputs(seed: int = 0) -> dict:
    key_list = jax.random.split(jax.random.key(seed), 14)
    return {
        "tokens": draw_tokens(jax.random.fold_in(key_list[13], 71), 0),
        "out_grad": scatter_about(key_list[1], (FRAMES, DEPTH, CELLS, C), 1.0, 6.0, ((0, 4), (1, 8))),
        "first_gain": jnp.clip(1.0 + 0.15 * jax.random.normal(key_list[2], (C,), jnp.float32), 0.25, 1.75),
        "depth_qkv": scatter_about(key_list[3], (C, 3 * C), C ** -0.5, 0.3125),
        "depth_out": scatter_about(key_list[4], (C, C), C ** -0.5, 0.3125),
        "time_qkv": scatter_about(key_list[5], (C, 3 * C), C ** -0.5, 0.3125),
        "time_out": scatter_about(key_list[6], (C, C), C ** -0.5, 0.3125),
        "second_gain": jnp.clip(1.0 + 0.15 * jax.random.normal(key_list[7], (C,), jnp.float32), 0.25, 1.75),
        "up_weight": scatter_about(key_list[8], (C, HID), C ** -0.5, 0.3125),
        "spatial_kernel": scatter_about(key_list[9], (3, 3, 3, HID), 27 ** -0.5, 1.25, (), jnp.float32),
        "down_weight": scatter_about(key_list[10], (HID, C), HID ** -0.5, 0.15625),
        "depth_scale": jnp.clip(jnp.exp(jax.random.uniform(key_list[11], (NH,), jnp.float32, math.log(2.0), math.log(10.0))), 2.0, 10.0),
        "time_scale": jnp.clip(jnp.exp(jax.random.uniform(key_list[12], (NH,), jnp.float32, math.log(2.0), math.log(10.0))), 2.0, 10.0),
    }


def rounded(values):
    return lax.optimization_barrier(values.astype(jnp.bfloat16))

def normalize(values, gain):
    centered = values - lax.optimization_barrier(jnp.mean(values, axis=-1, keepdims=True))
    spread = lax.optimization_barrier(jnp.mean(centered * centered, axis=-1, keepdims=True))
    return centered * lax.rsqrt(spread + 1e-05) * gain

def project(left, weight):
    return jnp.dot(left, weight, preferred_element_type=jnp.float32)

def back_project(grads, weight):
    return lax.dot_general(grads, weight, (((grads.ndim - 1,), (1,)), ((), ())), preferred_element_type=jnp.float32)

def weight_grad(left, grads):
    lead = tuple(range(left.ndim - 1))
    return lax.dot_general(left, grads, ((lead, lead), ((), ())), preferred_element_type=jnp.float32)

def attend(fields, scale):
    width = fields.shape[-1] // 3
    heads = scale.shape[0]
    split_shape = fields.shape[:-1] + (heads, width // heads)
    query = fields[..., :width].reshape(split_shape)
    keyed = fields[..., width:2 * width].reshape(split_shape)
    valued = fields[..., 2 * width:].reshape(split_shape)
    query = query * lax.rsqrt(lax.optimization_barrier(jnp.sum(query * query, axis=-1, keepdims=True)) + 1e-06)
    keyed = keyed * lax.rsqrt(lax.optimization_barrier(jnp.sum(keyed * keyed, axis=-1, keepdims=True)) + 1e-06)
    scores = jnp.einsum('plbhd,pmbhd->pbhlm', query, keyed, precision=lax.Precision.HIGHEST)
    scores = scores * scale[:, None, None]
    weights = jnp.exp(scores)
    weights = weights / lax.optimization_barrier(jnp.sum(weights, axis=-1, keepdims=True))
    mixed = jnp.einsum('pbhlm,pmbhd->plbhd', weights, valued, precision=lax.Precision.HIGHEST)
    return mixed.reshape(fields.shape[:-1] + (width,))

def activate(values):
    return 0.5 * values * (1.0 + jnp.tanh(0.7978845608 * (values + 0.044715 * values * values * values)))

def filter_forward(padded, kernel):
    depth = padded.shape[1] - 2
    rows = padded.shape[2] - 2
    cols = padded.shape[3] - 2
    total = jnp.zeros((padded.shape[0], depth, rows, cols, padded.shape[4]), jnp.float32)
    for depth_off in range(3):
        for row_off in range(3):
            for col_off in range(3):
                window = padded[:, depth_off:depth_off + depth, row_off:row_off + rows, col_off:col_off + cols]
                total = total + kernel[depth_off, row_off, col_off] * window.astype(jnp.float32)
    return total

def filter_backward(grad_pad, kernel):
    depth = grad_pad.shape[1] - 2
    rows = grad_pad.shape[2] - 2
    cols = grad_pad.shape[3] - 2
    total = jnp.zeros((grad_pad.shape[0], depth, rows, cols, grad_pad.shape[4]), jnp.float32)
    for depth_off in range(3):
        for row_off in range(3):
            for col_off in range(3):
                window = grad_pad[:, 2 - depth_off:2 - depth_off + depth, 2 - row_off:2 - row_off + rows, 2 - col_off:2 - col_off + cols]
                total = total + kernel[depth_off, row_off, col_off] * window.astype(jnp.float32)
    return total

def kernel_terms(padded, grads):
    depth = grads.shape[1]
    rows = grads.shape[2]
    cols = grads.shape[3]
    grads_wide = grads.astype(jnp.float32)
    terms = []
    for depth_off in range(3):
        for row_off in range(3):
            for col_off in range(3):
                window = padded[:, depth_off:depth_off + depth, row_off:row_off + rows, col_off:col_off + cols]
                terms.append(lax.optimization_barrier(jnp.sum(window.astype(jnp.float32) * grads_wide, axis=(0, 1, 2, 3))))
    return jnp.stack(terms).reshape(3, 3, 3, grads.shape[4])

def feed_forward(middle, out_grad, second_gain, up_weight, spatial_kernel, down_weight):
    frames, depth, cells, width = middle.shape
    middle_wide = middle.astype(jnp.float32)
    norm_second = rounded(normalize(middle_wide, second_gain))
    hidden = rounded(project(norm_second, up_weight))
    shaped = hidden.reshape(frames, depth, PH, PW, -1)
    padded = jnp.pad(shaped, ((0, 0), (1, 1), (1, 1), (1, 1), (0, 0)))
    filtered = filter_forward(padded, spatial_kernel)
    activated, act_back = jax.vjp(activate, filtered)
    active = rounded(activated).reshape(frames, depth, cells, -1)
    block_out = rounded(middle_wide + project(active, down_weight))
    down_grad = weight_grad(active, out_grad)
    active_grad = back_project(out_grad, down_weight)
    filtered_grad = rounded(act_back(active_grad.reshape(filtered.shape))[0])
    grad_pad = jnp.pad(filtered_grad, ((0, 0), (1, 1), (1, 1), (1, 1), (0, 0)))
    hidden_grad = rounded(filter_backward(grad_pad, spatial_kernel)).reshape(frames, depth, cells, -1)
    kernel_grad = kernel_terms(padded, filtered_grad)
    up_grad = weight_grad(norm_second, hidden_grad)
    second_back = back_project(hidden_grad, up_weight)
    norm_out, norm_back = jax.vjp(normalize, middle_wide, second_gain)
    middle_part, second_gain_grad = norm_back(second_back)
    middle_grad = out_grad.astype(jnp.float32) + middle_part
    return (block_out, middle_grad, up_grad, kernel_grad, down_grad, second_gain_grad)

def reference(tokens, out_grad, first_gain, depth_qkv, depth_out, time_qkv, time_out, second_gain, up_weight, spatial_kernel, down_weight, depth_scale, time_scale):
    frames, depth, cells, width = tokens.shape
    base = tokens.astype(jnp.float32)
    norm_first = rounded(normalize(base, first_gain))
    depth_fields = rounded(project(norm_first, depth_qkv))
    depth_wide, depth_back = jax.vjp(attend, depth_fields.astype(jnp.float32), depth_scale)
    depth_mixed = rounded(depth_wide)
    time_fields = rounded(project(norm_first, time_qkv)).reshape(1, frames, depth * cells, 3 * width)
    time_wide, time_back = jax.vjp(attend, time_fields.astype(jnp.float32), time_scale)
    time_mixed = rounded(time_wide).reshape(frames, depth, cells, width)
    depth_branch = rounded(project(depth_mixed, depth_out))
    time_branch = rounded(project(time_mixed, time_out))
    middle = rounded(base + depth_branch.astype(jnp.float32) + time_branch.astype(jnp.float32))

    def one_frame(pair):
        results = feed_forward(pair[0][None], pair[1][None], second_gain, up_weight, spatial_kernel, down_weight)
        return (results[0][0], results[1][0], results[2], results[3], results[4], results[5])
    stacked = lax.map(one_frame, (middle, out_grad))
    block_out = stacked[0]
    middle_grad = stacked[1]
    up_grad = lax.optimization_barrier(jnp.sum(stacked[2], axis=0))
    kernel_grad = lax.optimization_barrier(jnp.sum(stacked[3], axis=0))
    down_grad = lax.optimization_barrier(jnp.sum(stacked[4], axis=0))
    second_gain_grad = lax.optimization_barrier(jnp.sum(stacked[5], axis=0))
    branch_grad = rounded(middle_grad)
    depth_out_grad = weight_grad(depth_mixed, branch_grad)
    time_out_grad = weight_grad(time_mixed, branch_grad)
    depth_mixed_grad = rounded(back_project(branch_grad, depth_out))
    time_mixed_grad = rounded(back_project(branch_grad, time_out)).reshape(1, frames, depth * cells, width)
    depth_fields_wide, depth_scale_grad = depth_back(depth_mixed_grad.astype(jnp.float32))
    depth_fields_grad = rounded(depth_fields_wide)
    time_fields_wide, time_scale_grad = time_back(time_mixed_grad.astype(jnp.float32))
    time_fields_grad = rounded(time_fields_wide).reshape(frames, depth, cells, 3 * width)
    depth_qkv_grad = weight_grad(norm_first, depth_fields_grad)
    time_qkv_grad = weight_grad(norm_first, time_fields_grad)
    first_back = rounded(back_project(depth_fields_grad, depth_qkv)).astype(jnp.float32) + rounded(back_project(time_fields_grad, time_qkv)).astype(jnp.float32)
    norm_out, first_norm_back = jax.vjp(normalize, base, first_gain)
    base_grad, first_gain_grad = first_norm_back(first_back)
    input_grad = (middle_grad + base_grad).astype(jnp.bfloat16)
    factor = 1.0 / math.sqrt(frames * depth * cells)
    return (block_out, input_grad, depth_qkv_grad * factor, depth_out_grad * factor, time_qkv_grad * factor, time_out_grad * factor, up_grad * factor, kernel_grad * factor, down_grad * factor, first_gain_grad * factor, second_gain_grad * factor, depth_scale_grad * factor, time_scale_grad * factor)
```

```python
import functools
import math

import jax
import jax.numpy as jnp
import numpy as np
from jax import lax
from jax.experimental import pallas as pl
from jax.experimental.pallas import tpu as pltpu
from jax.sharding import PartitionSpec as P

PH = 6
PW = 24
LANES = 128
CHUNK = 256
BF = jnp.bfloat16
F32 = jnp.float32
MESH = pl.DeviceIdType.MESH
VMEM_BYTES = 56 * 1024 * 1024

VM = pl.BlockSpec(memory_space=pltpu.VMEM)
SM = pl.BlockSpec(memory_space=pltpu.SMEM)


def dot(left, right):
    return jnp.dot(left, right, preferred_element_type=F32)


def dot_nt(left, right):
    return lax.dot_general(left, right, (((1,), (1,)), ((), ())), preferred_element_type=F32)


def dot_tn(left, right):
    return lax.dot_general(left, right, (((0,), (0,)), ((), ())), preferred_element_type=F32)


def params(**more):
    return pltpu.CompilerParams(vmem_limit_bytes=VMEM_BYTES, **more)


def standard(values):
    centered = values - jnp.mean(values, axis=-1, keepdims=True)
    spread = jnp.mean(centered * centered, axis=-1, keepdims=True)
    inverse = lax.rsqrt(spread + 1e-05)
    return centered * inverse, inverse


def norm_back(values, gain, back):
    high, inverse = standard(values)
    inner = back * gain
    part = inner - jnp.mean(inner, axis=-1, keepdims=True)
    part = part - high * jnp.mean(inner * high, axis=-1, keepdims=True)
    return part * inverse, jnp.sum(back * high, axis=0, keepdims=True)


def exchange_kernel(nd, nt, sd, st, rd, rt, send_d, recv_d, send_t, recv_t):
    d = lax.axis_index("dev")
    t = lax.axis_index("ta")
    barrier = pltpu.get_barrier_semaphore()
    for off in range(1, nd):
        peer = lax.rem(d + off, nd)
        pl.semaphore_signal(barrier, inc=1, device_id=(peer, t), device_id_type=MESH)
    for off in range(1, nt):
        peer = lax.rem(t + off, nt)
        pl.semaphore_signal(barrier, inc=1, device_id=(d, peer), device_id_type=MESH)
    pl.semaphore_wait(barrier, nd + nt - 2)
    copies = []
    for off in range(1, nt):
        peer = lax.rem(t + off, nt)
        copies.append(
            pltpu.make_async_remote_copy(
                src_ref=st.at[peer],
                dst_ref=rt.at[t],
                send_sem=send_t.at[off - 1],
                recv_sem=recv_t.at[off - 1],
                device_id=(d, peer),
                device_id_type=MESH,
            )
        )
    for off in range(1, nd):
        peer = lax.rem(d + off, nd)
        copies.append(
            pltpu.make_async_remote_copy(
                src_ref=sd.at[peer],
                dst_ref=rd.at[d],
                send_sem=send_d.at[off - 1],
                recv_sem=recv_d.at[off - 1],
                device_id=(peer, t),
                device_id_type=MESH,
            )
        )
    for copy in copies:
        copy.start()
    rd[d] = sd[d]
    rt[t] = st[t]
    for copy in copies:
        copy.wait()


def exchange(send_d, send_t, nd, nt):
    width = send_d.shape[-1]
    sd = send_d.reshape(nd, -1, width)
    st = send_t.reshape(nt, -1, width)
    rd, rt = pl.pallas_call(
        functools.partial(exchange_kernel, nd, nt),
        out_shape=(
            jax.ShapeDtypeStruct(sd.shape, sd.dtype),
            jax.ShapeDtypeStruct(st.shape, st.dtype),
        ),
        in_specs=[VM, VM],
        out_specs=(VM, VM),
        scratch_shapes=[
            pltpu.SemaphoreType.DMA((nd - 1,)),
            pltpu.SemaphoreType.DMA((nd - 1,)),
            pltpu.SemaphoreType.DMA((nt - 1,)),
            pltpu.SemaphoreType.DMA((nt - 1,)),
        ],
        compiler_params=pltpu.CompilerParams(
            collective_id=0, has_side_effects=True, vmem_limit_bytes=VMEM_BYTES
        ),
        name="exchange",
    )(sd, st)
    return rd.reshape(send_d.shape), rt.reshape(send_t.shape)


def first_kernel(tokens, gain, pd, pt, out_d, out_t):
    high, _ = standard(tokens[...].astype(F32))
    normed = (high * gain[...]).astype(BF)
    out_d[...] = dot(pd[...], normed).astype(BF)
    out_t[...] = dot(pt[...], normed).astype(BF)


def attend_forward(x, qkv, out, mask, scale, fields, mixed_t, branch, qs, ks, vt):
    rows, width = x.shape
    heads = scale.shape[0]
    size = width // heads
    full = dot(x[...], qkv[...]).astype(BF)
    fields[...] = full
    wide = full.astype(F32)
    qs[...] = wide[:, :width].T
    ks[...] = wide[:, width : 2 * width]
    vt[...] = wide[:, 2 * width :].T.astype(BF)
    for head in range(heads):
        part = slice(head * size, (head + 1) * size)
        query = qs[part, :]
        factor = lax.rsqrt(jnp.sum(query * query, axis=0, keepdims=True) + 1e-06) * scale[head]
        query = query.astype(BF)
        keyed = ks[:, part]
        keyed = keyed * lax.rsqrt(jnp.sum(keyed * keyed, axis=1, keepdims=True) + 1e-06)
        keyed = keyed.astype(BF)
        valued = vt[part, :]
        for start in range(0, rows, LANES):
            cols = slice(start, start + LANES)
            score = dot(keyed, query[:, cols]) * factor[:, cols]
            raised = jnp.exp(score) * mask[:, cols]
            total = jnp.sum(raised, axis=0, keepdims=True)
            mixed = dot(valued, raised.astype(BF)) / total
            mixed_t[part, cols] = mixed.astype(BF)
    mixed = mixed_t[...].astype(F32).T.astype(BF)
    branch[...] = dot(mixed, out[...]).astype(BF)


def attention_kernel(
    scale_d, scale_t, xd, xt, qkv_d, out_d, qkv_t, out_t, mask_d, mask_t,
    fields_d, mixed_d, branch_d, fields_t, mixed_t, branch_t, qs, ks, vt, qs2, ks2, vt2,
):
    attend_forward(xd, qkv_d, out_d, mask_d, scale_d, fields_d, mixed_d, branch_d, qs, ks, vt)
    attend_forward(xt, qkv_t, out_t, mask_t, scale_t, fields_t, mixed_t, branch_t, qs2, ks2, vt2)


def attend_backward(
    x, grads, fields, mixed_t, qkv, out, mask, scale, factor,
    first, qkv_grad, out_grad, scale_grad, qt, kt, gt, natural, dqt, dfields,
):
    rows, width = x.shape
    heads = scale.shape[0]
    size = width // heads
    cot = grads[...]
    out_grad[...] = (dot(mixed_t[...], cot) * factor).astype(BF)
    heads_grad = dot_nt(cot, out[...]).astype(BF)
    gt[...] = heads_grad.astype(F32).T.astype(BF)
    wide = fields[...].astype(F32)
    natural[:, :width] = wide[:, : width]
    natural[:, width : 2 * width] = wide[:, width : 2 * width]
    natural[:, 2 * width :] = heads_grad.astype(F32)
    qt[...] = wide[:, :width].T
    kt[...] = wide[:, width : 2 * width].T
    for head in range(heads):
        lo, hi = head * size, (head + 1) * size
        part = slice(lo, hi)
        by = scale[head]
        query = qt[part, :]
        inverse_q = lax.rsqrt(jnp.sum(query * query, axis=0, keepdims=True) + 1e-06)
        query_t = query * inverse_q
        query = query.astype(BF)
        query_n = natural[:, lo:hi]
        query_n = query_n * lax.rsqrt(jnp.sum(query_n * query_n, axis=1, keepdims=True) + 1e-06)
        query_n = query_n.astype(BF)
        keyed = natural[:, width + lo : width + hi]
        inverse_k = lax.rsqrt(jnp.sum(keyed * keyed, axis=1, keepdims=True) + 1e-06)
        keyed = keyed * inverse_k
        keyed_b = keyed.astype(BF)
        key_t = kt[part, :]
        key_t = key_t * lax.rsqrt(jnp.sum(key_t * key_t, axis=0, keepdims=True) + 1e-06)
        key_t = key_t.astype(BF)
        valued = fields[:, 2 * width + lo : 2 * width + hi]
        weights, slopes = [], []
        for start in range(0, rows, LANES):
            cols = slice(start, start + LANES)
            inverse = inverse_q[:, cols]
            cosine = dot(keyed_b, query[:, cols]) * inverse
            raised = jnp.exp(cosine * by) * mask[:, cols]
            weight = raised * (1.0 / jnp.sum(raised, axis=0, keepdims=True))
            slope = dot(valued, gt[part, cols])
            delta = jnp.sum(weight * slope, axis=0, keepdims=True)
            slope = weight * (slope - delta)
            scale_grad[head : head + 1, cols] = jnp.sum(slope * cosine, axis=0, keepdims=True)
            slope = (slope * by).astype(BF)
            weights.append(weight.astype(BF))
            slopes.append(slope)
            back = dot(key_t, slope)
            unit = query_t[:, cols]
            back = back - unit * jnp.sum(back * unit, axis=0, keepdims=True)
            dqt[part, cols] = back * inverse
        weight = jnp.concatenate(weights, axis=1)
        slope = jnp.concatenate(slopes, axis=1)
        dfields[:, 2 * width + lo : 2 * width + hi] = dot(
            weight, natural[:, 2 * width + lo : 2 * width + hi].astype(BF)
        )
        back = dot(slope, query_n)
        back = back - keyed * jnp.sum(back * keyed, axis=1, keepdims=True)
        dfields[:, width + lo : width + hi] = back * inverse_k
    dfields[:, :width] = dqt[...].T
    narrow = dfields[...].astype(BF)
    first[...] = dot_nt(narrow, qkv[...]).astype(BF)
    turned = x[...].astype(F32).T.astype(BF)
    qkv_grad[...] = (dot(turned, narrow) * factor).astype(BF)


def attention_back_kernel(
    factor, scale_d, scale_t, xd, xt, gd, gt_, fields_d, fields_t, mixed_d, mixed_t,
    qkv_d, out_d, qkv_t, out_t, mask_d, mask_t,
    first_d, first_t, qkv_grad_d, qkv_grad_t, out_grad_d, out_grad_t, sg_d, sg_t, *scratch,
):
    attend_backward(
        xd, gd, fields_d, mixed_d, qkv_d, out_d, mask_d, scale_d, factor,
        first_d, qkv_grad_d, out_grad_d, sg_d, *scratch[:6],
    )
    attend_backward(
        xt, gt_, fields_t, mixed_t, qkv_t, out_t, mask_t, scale_t, factor,
        first_t, qkv_grad_t, out_grad_t, sg_t, *scratch[6:],
    )


def middle_kernel(tokens, bd, bt, pdt, ptt, middle):
    depth_part = dot(pdt[...], bd[...])
    time_part = dot(ptt[...], bt[...])
    middle[...] = (tokens[...].astype(F32) + depth_part + time_part).astype(BF)


def shifted(values):
    rows = values.shape[0]
    column = lax.broadcasted_iota(jnp.int32, values.shape, 0) % PW
    left = jnp.where(column == 0, 0.0, pltpu.roll(values, 1, 0))
    right = jnp.where(column == PW - 1, 0.0, pltpu.roll(values, rows - 1, 0))
    return (left, values, right)


def fill_windows(windows, slab, values):
    cells = values.shape[0]
    for off, moved in enumerate(shifted(values)):
        windows[off, slab, PW : PW + cells, :] = moved


def clear_rims(windows, cells):
    slabs = windows.shape[1]
    blank = jnp.zeros((PW, windows.shape[3]), F32)
    for off in range(3):
        for slab in range(slabs):
            windows[off, slab, 0:PW, :] = blank
            windows[off, slab, PW + cells : 2 * PW + cells, :] = blank


def feed_kernel(
    factor, slabs, cells, low, mid, high, gain, og, up, kernel, down,
    fg, block_out, down_grad, kernel_grad, normed_out, normed, windows, total, active,
):
    step = pl.program_id(0)
    own = slabs * cells

    @pl.when(step == 0)
    def _():
        for start, source in ((0, low), (cells, mid), (cells + own, high)):
            values = source[...].astype(F32)
            unit, _ = standard(values)
            normed[start : start + values.shape[0], :] = (unit * gain[...]).astype(BF)
        normed_out[...] = normed[cells : cells + own, :]
        total[...] = mid[...].astype(F32)
        clear_rims(windows, cells)

    for slab in range(slabs + 2):
        hidden = dot(normed[slab * cells : (slab + 1) * cells, :], up[...])
        fill_windows(windows, slab, hidden.astype(BF).astype(F32))
    for slab in range(slabs):
        rows = slice(slab * cells, (slab + 1) * cells)
        slope = dot_nt(og[rows, :], down[...])
        for start in range(0, CHUNK, LANES):
            lanes = slice(start, start + LANES)
            value = jnp.zeros((cells, LANES), F32)
            for a in range(3):
                for b in range(3):
                    for e in range(3):
                        tap = a * 9 + b * 3 + e
                        window = windows[e, slab + a, b * PW : b * PW + cells, lanes]
                        value = value + kernel[tap : tap + 1, lanes] * window
            square = value * value
            bent = jnp.tanh(0.7978845608 * value * (1.0 + 0.044715 * square))
            half = 0.5 * (1.0 + bent)
            active[rows, lanes] = (value * half).astype(BF)
            tilt = half + 0.5 * value * (1.0 - bent * bent) * (
                0.7978845608 * (1.0 + 3.0 * 0.044715 * square)
            )
            fg[rows, lanes] = (slope[:, lanes] * tilt).astype(BF)
    for start in range(0, CHUNK, LANES):
        lanes = slice(start, start + LANES)
        for a in range(3):
            for b in range(3):
                for e in range(3):
                    tap = a * 9 + b * 3 + e
                    sums = jnp.zeros((8, LANES), F32)
                    for slab in range(slabs):
                        window = windows[e, slab + a, b * PW : b * PW + cells, lanes]
                        grads = fg[slab * cells : (slab + 1) * cells, lanes].astype(F32)
                        sums = sums + jnp.sum((window * grads).reshape(cells // 8, 8, LANES), axis=0)
                    kernel_grad[tap : tap + 1, lanes] = factor * jnp.sum(sums, axis=0, keepdims=True)
    total[...] += dot(active[...], down[...])
    down_grad[...] = (factor * dot_tn(active[...], og[...])).astype(BF)

    @pl.when(step == pl.num_programs(0) - 1)
    def _():
        block_out[...] = total[...].astype(BF)


def feed_back_kernel(
    factor, slabs, cells, low, fg, high, kernel, up, normed, mid, og, gain, pd, pt,
    up_grad, middle_grad, send_d, send_t, gain_grad, windows, turned, total, hidden,
):
    step = pl.program_id(0)

    @pl.when(step == 0)
    def _():
        total[...] = jnp.zeros_like(total)
        clear_rims(windows, cells)

    for slab in range(slabs + 2):
        if slab == 0:
            values = low[...]
        elif slab == slabs + 1:
            values = high[...]
        else:
            values = fg[(slab - 1) * cells : slab * cells, :]
        fill_windows(windows, slab, values.astype(F32))
    for slab in range(slabs):
        rows = slice(slab * cells, (slab + 1) * cells)
        for start in range(0, CHUNK, LANES):
            lanes = slice(start, start + LANES)
            value = jnp.zeros((cells, LANES), F32)
            for a in range(3):
                for b in range(3):
                    for e in range(3):
                        tap = (2 - a) * 9 + (2 - b) * 3 + (2 - e)
                        window = windows[e, slab + a, b * PW : b * PW + cells, lanes]
                        value = value + kernel[tap : tap + 1, lanes] * window
            hidden[rows, lanes] = value.astype(BF)
    total[...] += dot_nt(hidden[...], up[...])
    up_grad[...] = (factor * dot_tn(normed[...], hidden[...])).astype(BF)

    @pl.when(step == pl.num_programs(0) - 1)
    def _():
        part, gains = norm_back(mid[...].astype(F32), gain[...], total[...])
        gain_grad[...] = gains
        grads = og[...].astype(F32) + part
        middle_grad[...] = grads
        narrow = grads.astype(BF)
        send_d[...] = dot(pd[...], narrow).astype(BF)
        send_t[...] = dot(pt[...], narrow).astype(BF)


def last_kernel(tokens, gain, fd, ft, pdt, ptt, middle_grad, input_grad, gain_grad):
    back = dot(pdt[...], fd[...]) + dot(ptt[...], ft[...])
    part, gains = norm_back(tokens[...].astype(F32), gain[...], back)
    gain_grad[...] = gains
    input_grad[...] = (middle_grad[...] + part).astype(BF)


def placement(groups, slabs, cells):
    each = cells // groups
    padded = -(-each // 8) * 8
    while (slabs * padded) % 16 or (groups * slabs * padded) % LANES:
        padded += 8
    rows = groups * slabs * padded
    index = np.arange(rows)
    group, slab, cell = index // (slabs * padded), index // padded % slabs, index % padded
    token = slab * cells + group * each + cell
    hot = (token[:, None] == np.arange(slabs * cells)[None, :]) & (cell < each)[:, None]
    return padded, hot.astype(np.float32), cell, slab


def shape(dims, kind):
    return jax.ShapeDtypeStruct(dims, kind)


def local(
    tokens,
    out_grad,
    first_gain,
    depth_qkv,
    depth_out,
    time_qkv,
    time_out,
    second_gain,
    up_weight,
    spatial_kernel,
    down_weight,
    depth_scale,
    time_scale,
):
    frames, slabs, cells, width = tokens.shape
    assert frames == 1 and cells == PH * PW
    nd, nt = lax.axis_size("dev"), lax.axis_size("ta")
    heads = depth_scale.shape[0]
    hid = up_weight.shape[1]
    own = slabs * cells
    factor = 1.0 / math.sqrt(frames * slabs * cells * nd * nt)

    _, hot_d, cell_d, _ = placement(nd, slabs, cells)
    _, hot_t, cell_t, slab_t = placement(nt, slabs, cells)
    rows_d, rows_t = hot_d.shape[0], hot_t.shape[0]
    mask_d = jnp.asarray((cell_d[:, None] == cell_d[None, :]).astype(np.float32))
    same = (cell_t[:, None] == cell_t[None, :]) & (slab_t[:, None] == slab_t[None, :])
    mask_t = jnp.asarray(same.astype(np.float32))
    pd, pt = jnp.asarray(hot_d, BF), jnp.asarray(hot_t, BF)
    pdt, ptt = jnp.asarray(hot_d.T.copy(), BF), jnp.asarray(hot_t.T.copy(), BF)

    base = tokens.reshape(own, width)
    og = out_grad.reshape(own, width)
    gain1 = first_gain.reshape(1, width)
    gain2 = second_gain.reshape(1, width)
    taps = spatial_kernel.reshape(27, hid)

    send_d, send_t = pl.pallas_call(
        first_kernel,
        out_shape=(shape((rows_d, width), BF), shape((rows_t, width), BF)),
        in_specs=[VM] * 4,
        out_specs=(VM, VM),
        compiler_params=params(),
        name="first_norm",
    )(base, gain1, pd, pt)
    xd, xt = exchange(send_d, send_t, nd, nt)

    def trio(rows):
        return (
            shape((rows, 3 * width), BF),
            shape((width, rows), BF),
            shape((rows, width), BF),
        )

    def trio_scratch(rows):
        return [
            pltpu.VMEM((width, rows), F32),
            pltpu.VMEM((rows, width), F32),
            pltpu.VMEM((width, rows), BF),
        ]

    fields_d, mixed_d, branch_d, fields_t, mixed_t, branch_t = pl.pallas_call(
        attention_kernel,
        out_shape=trio(rows_d) + trio(rows_t),
        in_specs=[SM, SM] + [VM] * 8,
        out_specs=(VM,) * 6,
        scratch_shapes=trio_scratch(rows_d) + trio_scratch(rows_t),
        compiler_params=params(),
        name="attention",
    )(
        depth_scale, time_scale, xd, xt, depth_qkv, depth_out, time_qkv, time_out, mask_d, mask_t
    )
    bd, bt = exchange(branch_d, branch_t, nd, nt)
    middle = pl.pallas_call(
        middle_kernel,
        out_shape=shape((own, width), BF),
        in_specs=[VM] * 5,
        out_specs=VM,
        compiler_params=params(),
        name="middle",
    )(base, bd, bt, pdt, ptt)

    forward = [(i, i + 1) for i in range(nd - 1)]
    backward = [(target, source) for source, target in forward]
    low = lax.ppermute(middle[own - cells :], "dev", forward)
    high = lax.ppermute(middle[:cells], "dev", backward)

    def whole(dims):
        return pl.BlockSpec(dims, lambda c: (0, 0))

    def across(rows):
        return pl.BlockSpec((rows, CHUNK), lambda c: (0, c))

    def down_spec():
        return pl.BlockSpec((CHUNK, width), lambda c: (c, 0))

    fg, block_out, down_grad, kernel_grad, normed = pl.pallas_call(
        functools.partial(feed_kernel, factor, slabs, cells),
        grid=(hid // CHUNK,),
        out_shape=(
            shape((own, hid), BF),
            shape((own, width), BF),
            shape((hid, width), BF),
            shape((27, hid), F32),
            shape((own, width), BF),
        ),
        in_specs=[
            whole((cells, width)),
            whole((own, width)),
            whole((cells, width)),
            whole((1, width)),
            whole((own, width)),
            across(width),
            across(27),
            down_spec(),
        ],
        out_specs=(
            across(own),
            whole((own, width)),
            down_spec(),
            across(27),
            whole((own, width)),
        ),
        scratch_shapes=[
            pltpu.VMEM((own + 2 * cells, width), BF),
            pltpu.VMEM((3, slabs + 2, cells + 2 * PW, CHUNK), F32),
            pltpu.VMEM((own, width), F32),
            pltpu.VMEM((own, CHUNK), BF),
        ],
        compiler_params=params(dimension_semantics=("arbitrary",)),
        name="feed",
    )(low, middle, high, gain2, og, up_weight, taps, down_weight)

    fg_low = lax.ppermute(fg[own - cells :], "dev", forward)
    fg_high = lax.ppermute(fg[:cells], "dev", backward)

    up_grad, middle_grad, gsend_d, gsend_t, gain2_grad = pl.pallas_call(
        functools.partial(feed_back_kernel, factor, slabs, cells),
        grid=(hid // CHUNK,),
        out_shape=(
            shape((width, hid), BF),
            shape((own, width), F32),
            shape((rows_d, width), BF),
            shape((rows_t, width), BF),
            shape((1, width), F32),
        ),
        in_specs=[
            across(cells),
            across(own),
            across(cells),
            across(27),
            across(width),
            whole((own, width)),
            whole((own, width)),
            whole((own, width)),
            whole((1, width)),
            whole((rows_d, own)),
            whole((rows_t, own)),
        ],
        out_specs=(
            across(width),
            whole((own, width)),
            whole((rows_d, width)),
            whole((rows_t, width)),
            whole((1, width)),
        ),
        scratch_shapes=[
            pltpu.VMEM((3, slabs + 2, cells + 2 * PW, CHUNK), F32),
            pltpu.VMEM((width, own), BF),
            pltpu.VMEM((own, width), F32),
            pltpu.VMEM((own, CHUNK), BF),
        ],
        compiler_params=params(dimension_semantics=("arbitrary",)),
        name="feed_back",
    )(fg_low, fg, fg_high, taps, up_weight, normed, middle, og, gain2, pd, pt)

    gd, gt = exchange(gsend_d, gsend_t, nd, nt)

    def back_scratch(rows):
        return [
            pltpu.VMEM((width, rows), F32),
            pltpu.VMEM((width, rows), F32),
            pltpu.VMEM((width, rows), BF),
            pltpu.VMEM((rows, 3 * width), F32),
            pltpu.VMEM((width, rows), F32),
            pltpu.VMEM((rows, 3 * width), F32),
        ]

    (
        first_d, first_t, dqkv_grad, tqkv_grad, dout_grad, tout_grad, dsg, tsg,
    ) = pl.pallas_call(
        functools.partial(attention_back_kernel, factor),
        out_shape=(
            shape((rows_d, width), BF),
            shape((rows_t, width), BF),
            shape((width, 3 * width), BF),
            shape((width, 3 * width), BF),
            shape((width, width), BF),
            shape((width, width), BF),
            shape((heads, rows_d), F32),
            shape((heads, rows_t), F32),
        ),
        in_specs=[SM, SM] + [VM] * 14,
        out_specs=(VM,) * 8,
        scratch_shapes=back_scratch(rows_d) + back_scratch(rows_t),
        compiler_params=params(),
        name="attention_back",
    )(
        depth_scale, time_scale, xd, xt, gd, gt, fields_d, fields_t, mixed_d, mixed_t,
        depth_qkv, depth_out, time_qkv, time_out, mask_d, mask_t,
    )
    fd, ft = exchange(first_d, first_t, nd, nt)
    input_grad, gain1_grad = pl.pallas_call(
        last_kernel,
        out_shape=(shape((own, width), BF), shape((1, width), F32)),
        in_specs=[VM] * 7,
        out_specs=(VM, VM),
        compiler_params=params(),
        name="last_norm",
    )(base, gain1, fd, ft, pdt, ptt, middle_grad)

    axes = ("dev", "ta")
    down_sum = lax.psum(down_grad, axes)
    up_sum = lax.psum(up_grad, axes)
    dqkv_sum, tqkv_sum, dout_sum, tout_sum = lax.psum(
        (dqkv_grad, tqkv_grad, dout_grad, tout_grad), axes
    )
    small = jnp.concatenate(
        [
            kernel_grad.reshape(-1),
            gain1_grad.reshape(-1) * factor,
            gain2_grad.reshape(-1) * factor,
            jnp.sum(dsg, axis=1) * factor,
            jnp.sum(tsg, axis=1) * factor,
        ]
    )
    small = lax.psum(small, axes)
    at = 27 * hid
    return (
        block_out.reshape(tokens.shape),
        input_grad.reshape(tokens.shape),
        dqkv_sum.astype(F32),
        dout_sum.astype(F32),
        tqkv_sum.astype(F32),
        tout_sum.astype(F32),
        up_sum.astype(F32),
        small[:at].reshape(spatial_kernel.shape),
        down_sum.astype(F32),
        small[at : at + width],
        small[at + width : at + 2 * width],
        small[at + 2 * width : at + 2 * width + heads],
        small[at + 2 * width + heads :],
    )


def solution(mesh):
    lead = P("ta", "dev", None, None)
    return jax.shard_map(
        local,
        mesh=mesh,
        in_specs=(lead, lead) + (P(),) * 11,
        out_specs=(lead, lead) + (P(),) * 11,
        check_vma=False,
    )
```

```python
import functools
import math

import jax
import jax.numpy as jnp
import numpy as np
from jax import lax
from jax.experimental import pallas as pl
from jax.experimental.pallas import tpu as pltpu
from jax.sharding import PartitionSpec as P

PH = 6
PW = 24
LANES = 128
CHUNK = 256
BF = jnp.bfloat16
F32 = jnp.float32
MESH = pl.DeviceIdType.MESH
VMEM_BYTES = 56 * 1024 * 1024

VM = pl.BlockSpec(memory_space=pltpu.VMEM)
SM = pl.BlockSpec(memory_space=pltpu.SMEM)


def dot(left, right):
    return jnp.dot(left, right, preferred_element_type=F32)


def dot_nt(left, right):
    return lax.dot_general(left, right, (((1,), (1,)), ((), ())), preferred_element_type=F32)


def dot_tn(left, right):
    return lax.dot_general(left, right, (((0,), (0,)), ((), ())), preferred_element_type=F32)


def params(**more):
    return pltpu.CompilerParams(vmem_limit_bytes=VMEM_BYTES, **more)


def standard(values):
    centered = values - jnp.mean(values, axis=-1, keepdims=True)
    spread = jnp.mean(centered * centered, axis=-1, keepdims=True)
    inverse = lax.rsqrt(spread + 1e-05)
    return centered * inverse, inverse


def norm_back(values, gain, back):
    high, inverse = standard(values)
    inner = back * gain
    part = inner - jnp.mean(inner, axis=-1, keepdims=True)
    part = part - high * jnp.mean(inner * high, axis=-1, keepdims=True)
    return part * inverse, jnp.sum(back * high, axis=0, keepdims=True)


def greet(barrier, nd, nt):
    d = lax.axis_index("dev")
    t = lax.axis_index("ta")
    for off in range(1, nd):
        peer = lax.rem(d + off, nd)
        pl.semaphore_signal(barrier, inc=1, device_id=(peer, t), device_id_type=MESH)
    for off in range(1, nt):
        peer = lax.rem(t + off, nt)
        pl.semaphore_signal(barrier, inc=1, device_id=(d, peer), device_id_type=MESH)


def block_copies(nd, nt, sd, st, rd, rt, send_d, recv_d, send_t, recv_t):
    d = lax.axis_index("dev")
    t = lax.axis_index("ta")
    copies = []
    for off in range(1, nt):
        peer = lax.rem(t + off, nt)
        copies.append(
            pltpu.make_async_remote_copy(
                src_ref=st.at[peer],
                dst_ref=rt.at[t],
                send_sem=send_t.at[off - 1],
                recv_sem=recv_t.at[off - 1],
                device_id=(d, peer),
                device_id_type=MESH,
            )
        )
    for off in range(1, nd):
        peer = lax.rem(d + off, nd)
        copies.append(
            pltpu.make_async_remote_copy(
                src_ref=sd.at[peer],
                dst_ref=rd.at[d],
                send_sem=send_d.at[off - 1],
                recv_sem=recv_d.at[off - 1],
                device_id=(peer, t),
                device_id_type=MESH,
            )
        )
    return copies


def exchange_kernel(nd, nt, sd, st, rd, rt, *sems):
    barrier = pltpu.get_barrier_semaphore()
    greet(barrier, nd, nt)
    pl.semaphore_wait(barrier, nd + nt - 2)
    copies = block_copies(nd, nt, sd, st, rd, rt, *sems)
    for copy in copies:
        copy.start()
    rd[lax.axis_index("dev")] = sd[lax.axis_index("dev")]
    rt[lax.axis_index("ta")] = st[lax.axis_index("ta")]
    for copy in copies:
        copy.wait()


def exchange(send_d, send_t, nd, nt):
    width = send_d.shape[-1]
    sd = send_d.reshape(nd, -1, width)
    st = send_t.reshape(nt, -1, width)
    rd, rt = pl.pallas_call(
        functools.partial(exchange_kernel, nd, nt),
        out_shape=(
            jax.ShapeDtypeStruct(sd.shape, sd.dtype),
            jax.ShapeDtypeStruct(st.shape, st.dtype),
        ),
        in_specs=[VM, VM],
        out_specs=(VM, VM),
        scratch_shapes=[
            pltpu.SemaphoreType.DMA((nd - 1,)),
            pltpu.SemaphoreType.DMA((nd - 1,)),
            pltpu.SemaphoreType.DMA((nt - 1,)),
            pltpu.SemaphoreType.DMA((nt - 1,)),
        ],
        compiler_params=pltpu.CompilerParams(
            collective_id=0, has_side_effects=True, vmem_limit_bytes=VMEM_BYTES
        ),
        name="exchange",
    )(sd, st)
    return rd.reshape(send_d.shape), rt.reshape(send_t.shape)


def first_kernel(tokens, gain, pd, pt, out_d, out_t):
    high, _ = standard(tokens[...].astype(F32))
    normed = (high * gain[...]).astype(BF)
    out_d[...] = dot(pd[...], normed).astype(BF)
    out_t[...] = dot(pt[...], normed).astype(BF)


def attend_forward(x, qkv, out, mask, scale, fields, mixed_t, branch, qs, ks, vt):
    rows, width = x.shape
    heads = scale.shape[0]
    size = width // heads
    full = dot(x[...], qkv[...]).astype(BF)
    fields[...] = full
    wide = full.astype(F32)
    qs[...] = wide[:, :width].T
    ks[...] = wide[:, width : 2 * width]
    vt[...] = wide[:, 2 * width :].T.astype(BF)
    for head in range(heads):
        part = slice(head * size, (head + 1) * size)
        query = qs[part, :]
        factor = lax.rsqrt(jnp.sum(query * query, axis=0, keepdims=True) + 1e-06) * scale[head]
        query = query.astype(BF)
        keyed = ks[:, part]
        keyed = keyed * lax.rsqrt(jnp.sum(keyed * keyed, axis=1, keepdims=True) + 1e-06)
        keyed = keyed.astype(BF)
        valued = vt[part, :]
        for start in range(0, rows, LANES):
            cols = slice(start, start + LANES)
            score = dot(keyed, query[:, cols]) * factor[:, cols]
            raised = jnp.exp(score) * mask[:, cols]
            total = jnp.sum(raised, axis=0, keepdims=True)
            mixed = dot(valued, raised.astype(BF)) / total
            mixed_t[part, cols] = mixed.astype(BF)
    mixed = mixed_t[...].astype(F32).T.astype(BF)
    branch[...] = dot(mixed, out[...]).astype(BF)


def attention_kernel(
    scale_d, scale_t, xd, xt, qkv_d, out_d, qkv_t, out_t, mask_d, mask_t,
    fields_d, mixed_d, branch_d, fields_t, mixed_t, branch_t, qs, ks, vt, qs2, ks2, vt2,
):
    attend_forward(xd, qkv_d, out_d, mask_d, scale_d, fields_d, mixed_d, branch_d, qs, ks, vt)
    attend_forward(xt, qkv_t, out_t, mask_t, scale_t, fields_t, mixed_t, branch_t, qs2, ks2, vt2)


def attend_backward(
    x, grads, fields, mixed_t, qkv, out, mask, scale, factor,
    first, qkv_grad, out_grad, scale_grad, gains, qt, kt, gt, natural, dqt, dfields,
):
    rows, width = x.shape
    heads = scale.shape[0]
    size = width // heads
    cot = grads[...]
    out_grad[...] = (dot(mixed_t[...], cot) * factor).astype(BF)
    heads_grad = dot_nt(cot, out[...]).astype(BF)
    gt[...] = heads_grad.astype(F32).T.astype(BF)
    wide = fields[...].astype(F32)
    natural[:, :width] = wide[:, : width]
    natural[:, width : 2 * width] = wide[:, width : 2 * width]
    natural[:, 2 * width :] = heads_grad.astype(F32)
    qt[...] = wide[:, :width].T
    kt[...] = wide[:, width : 2 * width].T
    for head in range(heads):
        lo, hi = head * size, (head + 1) * size
        part = slice(lo, hi)
        by = scale[head]
        query = qt[part, :]
        inverse_q = lax.rsqrt(jnp.sum(query * query, axis=0, keepdims=True) + 1e-06)
        query_t = query * inverse_q
        query = query.astype(BF)
        query_n = natural[:, lo:hi]
        query_n = query_n * lax.rsqrt(jnp.sum(query_n * query_n, axis=1, keepdims=True) + 1e-06)
        query_n = query_n.astype(BF)
        keyed = natural[:, width + lo : width + hi]
        inverse_k = lax.rsqrt(jnp.sum(keyed * keyed, axis=1, keepdims=True) + 1e-06)
        keyed = keyed * inverse_k
        keyed_b = keyed.astype(BF)
        key_t = kt[part, :]
        key_t = key_t * lax.rsqrt(jnp.sum(key_t * key_t, axis=0, keepdims=True) + 1e-06)
        key_t = key_t.astype(BF)
        valued = fields[:, 2 * width + lo : 2 * width + hi]
        weights, slopes = [], []
        for start in range(0, rows, LANES):
            cols = slice(start, start + LANES)
            inverse = inverse_q[:, cols]
            cosine = dot(keyed_b, query[:, cols]) * inverse
            raised = jnp.exp(cosine * by) * mask[:, cols]
            weight = raised * (1.0 / jnp.sum(raised, axis=0, keepdims=True))
            slope = dot(valued, gt[part, cols])
            delta = jnp.sum(weight * slope, axis=0, keepdims=True)
            slope = weight * (slope - delta)
            scale_grad[head : head + 1, cols] = jnp.sum(slope * cosine, axis=0, keepdims=True)
            slope = (slope * by).astype(BF)
            weights.append(weight.astype(BF))
            slopes.append(slope)
            back = dot(key_t, slope)
            unit = query_t[:, cols]
            back = back - unit * jnp.sum(back * unit, axis=0, keepdims=True)
            dqt[part, cols] = back * inverse
        weight = jnp.concatenate(weights, axis=1)
        slope = jnp.concatenate(slopes, axis=1)
        dfields[:, 2 * width + lo : 2 * width + hi] = dot(
            weight, natural[:, 2 * width + lo : 2 * width + hi].astype(BF)
        )
        back = dot(slope, query_n)
        back = back - keyed * jnp.sum(back * keyed, axis=1, keepdims=True)
        dfields[:, width + lo : width + hi] = back * inverse_k
    dfields[:, :width] = dqt[...].T
    narrow = dfields[...].astype(BF)
    back = dot_nt(narrow, qkv[...]).astype(BF)
    first[...] = back
    gains[...] += jnp.sum(back.astype(F32) * x[...].astype(F32), axis=0, keepdims=True)
    turned = x[...].astype(F32).T.astype(BF)
    qkv_grad[...] = (dot(turned, narrow) * factor).astype(BF)


def attention_back_kernel(
    factor, scale_d, scale_t, xd, xt, gd, gt_, fields_d, fields_t, mixed_d, mixed_t,
    qkv_d, out_d, qkv_t, out_t, mask_d, mask_t,
    first_d, first_t, qkv_grad_d, qkv_grad_t, out_grad_d, out_grad_t, sg_d, sg_t, gains, *scratch,
):
    gains[...] = jnp.zeros_like(gains)
    attend_backward(
        xd, gd, fields_d, mixed_d, qkv_d, out_d, mask_d, scale_d, factor,
        first_d, qkv_grad_d, out_grad_d, sg_d, gains, *scratch[:6],
    )
    attend_backward(
        xt, gt_, fields_t, mixed_t, qkv_t, out_t, mask_t, scale_t, factor,
        first_t, qkv_grad_t, out_grad_t, sg_t, gains, *scratch[6:],
    )


def middle_kernel(tokens, bd, bt, pdt, ptt, middle):
    depth_part = dot(pdt[...], bd[...])
    time_part = dot(ptt[...], bt[...])
    middle[...] = (tokens[...].astype(F32) + depth_part + time_part).astype(BF)


def shifted(values):
    rows = values.shape[0]
    column = lax.broadcasted_iota(jnp.int32, values.shape, 0) % PW
    left = jnp.where(column == 0, 0.0, pltpu.roll(values, 1, 0))
    right = jnp.where(column == PW - 1, 0.0, pltpu.roll(values, rows - 1, 0))
    return (left, values, right)


def fill_windows(windows, slab, values):
    cells = values.shape[0]
    for off, moved in enumerate(shifted(values)):
        windows[off, slab, PW : PW + cells, :] = moved


def clear_rims(windows, cells):
    slabs = windows.shape[1]
    blank = jnp.zeros((PW, windows.shape[3]), F32)
    for off in range(3):
        for slab in range(slabs):
            windows[off, slab, 0:PW, :] = blank
            windows[off, slab, PW + cells : 2 * PW + cells, :] = blank


def feed_kernel(
    factor, slabs, cells, low, mid, high, gain, og, up, kernel, down,
    fg, block_out, down_grad, kernel_grad, normed_out, normed, windows, total, active,
):
    step = pl.program_id(0)
    own = slabs * cells

    @pl.when(step == 0)
    def _():
        for start, source in ((0, low), (cells, mid), (cells + own, high)):
            values = source[...].astype(F32)
            unit, _ = standard(values)
            normed[start : start + values.shape[0], :] = (unit * gain[...]).astype(BF)
        normed_out[...] = normed[cells : cells + own, :]
        total[...] = mid[...].astype(F32)
        clear_rims(windows, cells)

    for slab in range(slabs + 2):
        hidden = dot(normed[slab * cells : (slab + 1) * cells, :], up[...])
        fill_windows(windows, slab, hidden.astype(BF).astype(F32))
    for slab in range(slabs):
        rows = slice(slab * cells, (slab + 1) * cells)
        slope = dot_nt(og[rows, :], down[...])
        for start in range(0, CHUNK, LANES):
            lanes = slice(start, start + LANES)
            value = jnp.zeros((cells, LANES), F32)
            for a in range(3):
                for b in range(3):
                    for e in range(3):
                        tap = a * 9 + b * 3 + e
                        window = windows[e, slab + a, b * PW : b * PW + cells, lanes]
                        value = value + kernel[tap : tap + 1, lanes] * window
            square = value * value
            bent = jnp.tanh(0.7978845608 * value * (1.0 + 0.044715 * square))
            half = 0.5 * (1.0 + bent)
            active[rows, lanes] = (value * half).astype(BF)
            tilt = half + 0.5 * value * (1.0 - bent * bent) * (
                0.7978845608 * (1.0 + 3.0 * 0.044715 * square)
            )
            fg[rows, lanes] = (slope[:, lanes] * tilt).astype(BF)
    for start in range(0, CHUNK, LANES):
        lanes = slice(start, start + LANES)
        for a in range(3):
            for b in range(3):
                for e in range(3):
                    tap = a * 9 + b * 3 + e
                    sums = jnp.zeros((8, LANES), F32)
                    for slab in range(slabs):
                        window = windows[e, slab + a, b * PW : b * PW + cells, lanes]
                        grads = fg[slab * cells : (slab + 1) * cells, lanes].astype(F32)
                        sums = sums + jnp.sum((window * grads).reshape(cells // 8, 8, LANES), axis=0)
                    kernel_grad[tap : tap + 1, lanes] = factor * jnp.sum(sums, axis=0, keepdims=True)
    total[...] += dot(active[...], down[...])
    down_grad[...] = (factor * dot_tn(active[...], og[...])).astype(BF)

    @pl.when(step == pl.num_programs(0) - 1)
    def _():
        block_out[...] = total[...].astype(BF)


def feed_back_kernel(
    factor, slabs, cells, low, fg, high, kernel, up, normed, mid, og, gain, pd, pt,
    up_grad, middle_grad, send_d, send_t, gain_grad, windows, turned, total, hidden,
):
    step = pl.program_id(0)

    @pl.when(step == 0)
    def _():
        total[...] = jnp.zeros_like(total)
        clear_rims(windows, cells)

    for slab in range(slabs + 2):
        if slab == 0:
            values = low[...]
        elif slab == slabs + 1:
            values = high[...]
        else:
            values = fg[(slab - 1) * cells : slab * cells, :]
        fill_windows(windows, slab, values.astype(F32))
    for slab in range(slabs):
        rows = slice(slab * cells, (slab + 1) * cells)
        for start in range(0, CHUNK, LANES):
            lanes = slice(start, start + LANES)
            value = jnp.zeros((cells, LANES), F32)
            for a in range(3):
                for b in range(3):
                    for e in range(3):
                        tap = (2 - a) * 9 + (2 - b) * 3 + (2 - e)
                        window = windows[e, slab + a, b * PW : b * PW + cells, lanes]
                        value = value + kernel[tap : tap + 1, lanes] * window
            hidden[rows, lanes] = value.astype(BF)
    total[...] += dot_nt(hidden[...], up[...])
    up_grad[...] = (factor * dot_tn(normed[...], hidden[...])).astype(BF)

    @pl.when(step == pl.num_programs(0) - 1)
    def _():
        part, gains = norm_back(mid[...].astype(F32), gain[...], total[...])
        gain_grad[...] = gains
        grads = og[...].astype(F32) + part
        middle_grad[...] = grads
        narrow = grads.astype(BF)
        send_d[...] = dot(pd[...], narrow).astype(BF)
        send_t[...] = dot(pt[...], narrow).astype(BF)


def last_kernel(tokens, gain, fd, ft, pdt, ptt, middle_grad, input_grad):
    back = dot(pdt[...], fd[...]) + dot(ptt[...], ft[...])
    part, _ = norm_back(tokens[...].astype(F32), gain[...], back)
    input_grad[...] = (middle_grad[...] + part).astype(BF)


def bits_of(count):
    assert count & (count - 1) == 0
    return count.bit_length() - 1


def orders_of(nd, nt):
    dev = [("dev", bit) for bit in range(bits_of(nd))]
    time = [("ta", bit) for bit in range(bits_of(nt))]
    head, near, far = dev[:1], dev[1:2], dev[2:]
    return (head + near + far + time, head + far + time + near, head + time + near + far)


def pack_plan(width, hid):
    blocks = [3, 3, 1, 1, hid // width]
    plan, at = [], 0
    for array, count in enumerate(blocks):
        for block in range(count):
            plan.append((array, block, at))
            at += width
    return plan, at


def sum_kernel(
    nd, nt, plan, at_down, qd, qt, od, ot, up, down, small, sd, st,
    big_out, small_out, rd, rt, big_sum, small_sum, big_in, small_in, send_sem, recv_sem, *sems,
):
    place = {"dev": lax.axis_index("dev"), "ta": lax.axis_index("ta")}
    orders = orders_of(nd, nt)
    stages = len(orders[0])
    width = down.shape[1]

    def digit(axis, bit):
        return lax.rem(place[axis] // (1 << bit), 2)

    def partner(axis, bit):
        moved = place[axis] + (1 - 2 * digit(axis, bit)) * (1 << bit)
        if axis == "dev":
            return (moved, place["ta"])
        return (place["dev"], moved)

    barrier = pltpu.get_barrier_semaphore()
    greet(barrier, nd, nt)

    arrays = (qd, qt, od, ot, up)
    for array, block, at in plan:
        big_sum[at : at + width, :] = arrays[array][:, block * width : (block + 1) * width]
    big_sum[at_down:, :] = down[...]
    small_sum[...] = small[...]
    rd[place["dev"]] = sd[place["dev"]]
    rt[place["ta"]] = st[place["ta"]]
    pl.semaphore_wait(barrier, nd + nt - 2)
    blocks = block_copies(nd, nt, sd, st, rd, rt, *sems)
    for copy in blocks:
        copy.start()

    each = big_out.shape[0] // 3
    parts = []
    for index, order in enumerate(orders):
        parts.append((big_sum, big_out, big_in, order, index * each, each, 16))
    parts.append((small_sum, small_out, small_in, orders[1], 0, small_out.shape[0], 8))

    spans = []
    for target, result, landing, order, base, size, unit in parts:
        offs, sizes = [base], [size]
        for axis, bit in order:
            sizes.append(sizes[-1] // 2)
            offs.append(offs[-1] + digit(axis, bit) * sizes[-1])
        spans.append((offs, sizes))

    def reduce_copy(index, stage):
        target, result, landing, order, base, size, unit = parts[index]
        offs, sizes = spans[index]
        axis, bit = order[stage]
        half = sizes[stage + 1]
        away = offs[stage] + (1 - digit(axis, bit)) * half
        to = base + size - sizes[stage]
        return pltpu.make_async_remote_copy(
            src_ref=target.at[pl.ds(pl.multiple_of(away, unit), half), :],
            dst_ref=landing.at[pl.ds(to, half), :],
            send_sem=send_sem.at[index, stage],
            recv_sem=recv_sem.at[index, stage],
            device_id=partner(axis, bit),
            device_id_type=MESH,
        )

    def gather_copy(index, stage):
        target, result, landing, order, base, size, unit = parts[index]
        offs, sizes = spans[index]
        axis, bit = order[stage]
        rows = pl.ds(pl.multiple_of(offs[stage + 1], unit), sizes[stage + 1])
        return pltpu.make_async_remote_copy(
            src_ref=result.at[rows, :],
            dst_ref=result.at[rows, :],
            send_sem=send_sem.at[index, stages + stage],
            recv_sem=recv_sem.at[index, stages + stage],
            device_id=partner(axis, bit),
            device_id_type=MESH,
        )

    count = len(parts)
    flying = []
    for index in range(count):
        copy = reduce_copy(index, 0)
        copy.start()
        flying.append(copy)
    for stage in range(stages):
        for index in range(count):
            flying[index].wait()
            target, result, landing, order, base, size, unit = parts[index]
            offs, sizes = spans[index]
            half = sizes[stage + 1]
            to = base + size - sizes[stage]
            rows = pl.ds(pl.multiple_of(offs[stage + 1], unit), half)
            added = target[rows, :].astype(F32) + landing[to : to + half, :].astype(F32)
            if stage + 1 < stages:
                target[rows, :] = added.astype(target.dtype)
                copy = reduce_copy(index, stage + 1)
            else:
                result[rows, :] = added.astype(result.dtype)
                copy = gather_copy(index, stages - 1)
            copy.start()
            flying[index] = copy
    for stage in range(stages - 1, -1, -1):
        for index in range(count):
            flying[index].wait()
            if stage > 0:
                copy = gather_copy(index, stage - 1)
                copy.start()
                flying[index] = copy
    for copy in blocks:
        copy.wait()


def unpack_kernel(plan, at_down, big, qd, qt, od, ot, up, down):
    width = down.shape[1]
    arrays = (qd, qt, od, ot, up)
    for array, block, at in plan:
        arrays[array][:, block * width : (block + 1) * width] = big[at : at + width, :].astype(F32)
    down[...] = big[at_down:, :].astype(F32)


def sum_all(qd, qt, od, ot, up, down, small, send_d, send_t, nd, nt):
    width, hid = up.shape
    plan, at_down = pack_plan(width, hid)
    rows = at_down + hid
    devices = nd * nt
    stages = bits_of(devices)
    assert rows % (3 * 16 * devices) == 0
    unit = 8 * devices
    small_rows = -(-small.shape[0] // (unit * width)) * unit
    small = jnp.pad(small, (0, small_rows * width - small.shape[0])).reshape(small_rows, width)
    sd = send_d.reshape(nd, -1, width)
    st = send_t.reshape(nt, -1, width)
    big, small, rd, rt = pl.pallas_call(
        functools.partial(sum_kernel, nd, nt, plan, at_down),
        out_shape=(
            shape((rows, width), BF),
            shape((small_rows, width), F32),
            shape(sd.shape, BF),
            shape(st.shape, BF),
        ),
        in_specs=[VM] * 9,
        out_specs=(VM,) * 4,
        scratch_shapes=[
            pltpu.VMEM((rows, width), BF),
            pltpu.VMEM((small_rows, width), F32),
            pltpu.VMEM((rows, width), BF),
            pltpu.VMEM((small_rows, width), F32),
            pltpu.SemaphoreType.DMA((4, 2 * stages)),
            pltpu.SemaphoreType.DMA((4, 2 * stages)),
            pltpu.SemaphoreType.DMA((nd - 1,)),
            pltpu.SemaphoreType.DMA((nd - 1,)),
            pltpu.SemaphoreType.DMA((nt - 1,)),
            pltpu.SemaphoreType.DMA((nt - 1,)),
        ],
        compiler_params=params(collective_id=1, has_side_effects=True),
        name="sum_all",
    )(qd, qt, od, ot, up, down, small, sd, st)
    wide = pl.pallas_call(
        functools.partial(unpack_kernel, plan, at_down),
        out_shape=tuple(shape(value.shape, F32) for value in (qd, qt, od, ot, up, down)),
        in_specs=[VM],
        out_specs=(VM,) * 6,
        compiler_params=params(),
        name="unpack",
    )(big)
    return wide, small.reshape(-1), rd.reshape(send_d.shape), rt.reshape(send_t.shape)


def placement(groups, slabs, cells):
    each = cells // groups
    padded = -(-each // 8) * 8
    while (slabs * padded) % 16 or (groups * slabs * padded) % LANES:
        padded += 8
    rows = groups * slabs * padded
    index = np.arange(rows)
    group, slab, cell = index // (slabs * padded), index // padded % slabs, index % padded
    token = slab * cells + group * each + cell
    hot = (token[:, None] == np.arange(slabs * cells)[None, :]) & (cell < each)[:, None]
    return padded, hot.astype(np.float32), cell, slab


def shape(dims, kind):
    return jax.ShapeDtypeStruct(dims, kind)


def local(
    tokens,
    out_grad,
    first_gain,
    depth_qkv,
    depth_out,
    time_qkv,
    time_out,
    second_gain,
    up_weight,
    spatial_kernel,
    down_weight,
    depth_scale,
    time_scale,
):
    frames, slabs, cells, width = tokens.shape
    assert frames == 1 and cells == PH * PW
    nd, nt = lax.axis_size("dev"), lax.axis_size("ta")
    heads = depth_scale.shape[0]
    hid = up_weight.shape[1]
    own = slabs * cells
    factor = 1.0 / math.sqrt(frames * slabs * cells * nd * nt)

    _, hot_d, cell_d, _ = placement(nd, slabs, cells)
    _, hot_t, cell_t, slab_t = placement(nt, slabs, cells)
    rows_d, rows_t = hot_d.shape[0], hot_t.shape[0]
    mask_d = jnp.asarray((cell_d[:, None] == cell_d[None, :]).astype(np.float32))
    same = (cell_t[:, None] == cell_t[None, :]) & (slab_t[:, None] == slab_t[None, :])
    mask_t = jnp.asarray(same.astype(np.float32))
    pd, pt = jnp.asarray(hot_d, BF), jnp.asarray(hot_t, BF)
    pdt, ptt = jnp.asarray(hot_d.T.copy(), BF), jnp.asarray(hot_t.T.copy(), BF)

    base = tokens.reshape(own, width)
    og = out_grad.reshape(own, width)
    gain1 = first_gain.reshape(1, width)
    gain2 = second_gain.reshape(1, width)
    taps = spatial_kernel.reshape(27, hid)

    send_d, send_t = pl.pallas_call(
        first_kernel,
        out_shape=(shape((rows_d, width), BF), shape((rows_t, width), BF)),
        in_specs=[VM] * 4,
        out_specs=(VM, VM),
        compiler_params=params(),
        name="first_norm",
    )(base, gain1, pd, pt)
    xd, xt = exchange(send_d, send_t, nd, nt)

    def trio(rows):
        return (
            shape((rows, 3 * width), BF),
            shape((width, rows), BF),
            shape((rows, width), BF),
        )

    def trio_scratch(rows):
        return [
            pltpu.VMEM((width, rows), F32),
            pltpu.VMEM((rows, width), F32),
            pltpu.VMEM((width, rows), BF),
        ]

    fields_d, mixed_d, branch_d, fields_t, mixed_t, branch_t = pl.pallas_call(
        attention_kernel,
        out_shape=trio(rows_d) + trio(rows_t),
        in_specs=[SM, SM] + [VM] * 8,
        out_specs=(VM,) * 6,
        scratch_shapes=trio_scratch(rows_d) + trio_scratch(rows_t),
        compiler_params=params(),
        name="attention",
    )(
        depth_scale, time_scale, xd, xt, depth_qkv, depth_out, time_qkv, time_out, mask_d, mask_t
    )
    bd, bt = exchange(branch_d, branch_t, nd, nt)
    middle = pl.pallas_call(
        middle_kernel,
        out_shape=shape((own, width), BF),
        in_specs=[VM] * 5,
        out_specs=VM,
        compiler_params=params(),
        name="middle",
    )(base, bd, bt, pdt, ptt)

    forward = [(i, i + 1) for i in range(nd - 1)]
    backward = [(target, source) for source, target in forward]
    low = lax.ppermute(middle[own - cells :], "dev", forward)
    high = lax.ppermute(middle[:cells], "dev", backward)

    def whole(dims):
        return pl.BlockSpec(dims, lambda c: (0, 0))

    def across(rows):
        return pl.BlockSpec((rows, CHUNK), lambda c: (0, c))

    def down_spec():
        return pl.BlockSpec((CHUNK, width), lambda c: (c, 0))

    fg, block_out, down_grad, kernel_grad, normed = pl.pallas_call(
        functools.partial(feed_kernel, factor, slabs, cells),
        grid=(hid // CHUNK,),
        out_shape=(
            shape((own, hid), BF),
            shape((own, width), BF),
            shape((hid, width), BF),
            shape((27, hid), F32),
            shape((own, width), BF),
        ),
        in_specs=[
            whole((cells, width)),
            whole((own, width)),
            whole((cells, width)),
            whole((1, width)),
            whole((own, width)),
            across(width),
            across(27),
            down_spec(),
        ],
        out_specs=(
            across(own),
            whole((own, width)),
            down_spec(),
            across(27),
            whole((own, width)),
        ),
        scratch_shapes=[
            pltpu.VMEM((own + 2 * cells, width), BF),
            pltpu.VMEM((3, slabs + 2, cells + 2 * PW, CHUNK), F32),
            pltpu.VMEM((own, width), F32),
            pltpu.VMEM((own, CHUNK), BF),
        ],
        compiler_params=params(dimension_semantics=("arbitrary",)),
        name="feed",
    )(low, middle, high, gain2, og, up_weight, taps, down_weight)

    fg_low = lax.ppermute(fg[own - cells :], "dev", forward)
    fg_high = lax.ppermute(fg[:cells], "dev", backward)

    up_grad, middle_grad, gsend_d, gsend_t, gain2_grad = pl.pallas_call(
        functools.partial(feed_back_kernel, factor, slabs, cells),
        grid=(hid // CHUNK,),
        out_shape=(
            shape((width, hid), BF),
            shape((own, width), F32),
            shape((rows_d, width), BF),
            shape((rows_t, width), BF),
            shape((1, width), F32),
        ),
        in_specs=[
            across(cells),
            across(own),
            across(cells),
            across(27),
            across(width),
            whole((own, width)),
            whole((own, width)),
            whole((own, width)),
            whole((1, width)),
            whole((rows_d, own)),
            whole((rows_t, own)),
        ],
        out_specs=(
            across(width),
            whole((own, width)),
            whole((rows_d, width)),
            whole((rows_t, width)),
            whole((1, width)),
        ),
        scratch_shapes=[
            pltpu.VMEM((3, slabs + 2, cells + 2 * PW, CHUNK), F32),
            pltpu.VMEM((width, own), BF),
            pltpu.VMEM((own, width), F32),
            pltpu.VMEM((own, CHUNK), BF),
        ],
        compiler_params=params(dimension_semantics=("arbitrary",)),
        name="feed_back",
    )(fg_low, fg, fg_high, taps, up_weight, normed, middle, og, gain2, pd, pt)

    gd, gt = exchange(gsend_d, gsend_t, nd, nt)

    def back_scratch(rows):
        return [
            pltpu.VMEM((width, rows), F32),
            pltpu.VMEM((width, rows), F32),
            pltpu.VMEM((width, rows), BF),
            pltpu.VMEM((rows, 3 * width), F32),
            pltpu.VMEM((width, rows), F32),
            pltpu.VMEM((rows, 3 * width), F32),
        ]

    (
        first_d, first_t, dqkv_grad, tqkv_grad, dout_grad, tout_grad, dsg, tsg, gain1_part,
    ) = pl.pallas_call(
        functools.partial(attention_back_kernel, factor),
        out_shape=(
            shape((rows_d, width), BF),
            shape((rows_t, width), BF),
            shape((width, 3 * width), BF),
            shape((width, 3 * width), BF),
            shape((width, width), BF),
            shape((width, width), BF),
            shape((heads, rows_d), F32),
            shape((heads, rows_t), F32),
            shape((1, width), F32),
        ),
        in_specs=[SM, SM] + [VM] * 14,
        out_specs=(VM,) * 9,
        scratch_shapes=back_scratch(rows_d) + back_scratch(rows_t),
        compiler_params=params(),
        name="attention_back",
    )(
        depth_scale, time_scale, xd, xt, gd, gt, fields_d, fields_t, mixed_d, mixed_t,
        depth_qkv, depth_out, time_qkv, time_out, mask_d, mask_t,
    )
    small = jnp.concatenate(
        [
            kernel_grad.reshape(-1),
            gain1_part.reshape(-1) / first_gain * factor,
            gain2_grad.reshape(-1) * factor,
            jnp.sum(dsg, axis=1) * factor,
            jnp.sum(tsg, axis=1) * factor,
        ]
    )
    grads, small, fd, ft = sum_all(
        dqkv_grad, tqkv_grad, dout_grad, tout_grad, up_grad, down_grad, small,
        first_d, first_t, nd, nt,
    )
    input_grad = pl.pallas_call(
        last_kernel,
        out_shape=shape((own, width), BF),
        in_specs=[VM] * 7,
        out_specs=VM,
        compiler_params=params(),
        name="last_norm",
    )(base, gain1, fd, ft, pdt, ptt, middle_grad)

    dqkv_sum, tqkv_sum, dout_sum, tout_sum, up_sum, down_sum = grads
    at = 27 * hid
    return (
        block_out.reshape(tokens.shape),
        input_grad.reshape(tokens.shape),
        dqkv_sum,
        dout_sum,
        tqkv_sum,
        tout_sum,
        up_sum,
        small[:at].reshape(spatial_kernel.shape),
        down_sum,
        small[at : at + width],
        small[at + width : at + 2 * width],
        small[at + 2 * width : at + 2 * width + heads],
        small[at + 2 * width + heads : at + 2 * width + 2 * heads],
    )


def solution(mesh):
    lead = P("ta", "dev", None, None)
    return jax.shard_map(
        local,
        mesh=mesh,
        in_specs=(lead, lead) + (P(),) * 11,
        out_specs=(lead, lead) + (P(),) * 11,
        check_vma=False,
    )
```
